32 devices in a mesh: tm: 4 (over x, core), firm: 8 (over z, y).
Axes of the slice: x: 2, y: 2, z: 4, core: 2. Of those that a mesh axis runs over, the one named last changes fastest.
Arguments:
- features: bfloat16 [32, 2048, 256], P('tm', 'firm'), may hold values from -6 to 6
- supply_counts: int32 [32, 2048, 3, 256], P('tm', 'firm'), may hold values from 0 to 3
- bank_ids: int32 [32, 2048], P('tm', 'firm'), may hold values from 0 to 63
- sector_ids: int32 [32, 2048], P('tm', 'firm'), may hold values from 0 to 31
- bank_table: bfloat16 [64, 256], P('firm'), may hold values from -6 to 6
- sector_table: bfloat16 [32, 256], P('firm'), may hold values from -6 to 6
- w_supply: bfloat16 [256, 256], replicated, may hold values from -0.375 to 0.375
- w_query: bfloat16 [256, 256], replicated, may hold values from -0.375 to 0.375
- w_key: bfloat16 [256, 256], replicated, may hold values from -0.375 to 0.375
- w_value: bfloat16 [256, 256], replicated, may hold values from -0.375 to 0.375
- w_out: bfloat16 [256, 256], replicated, may hold values from -0.375 to 0.375
- w_in: bfloat16 [256, 1024], replicated, may hold values from -0.375 to 0.375
- w_down: bfloat16 [1024, 256], replicated, may hold values from -0.1875 to 0.1875
- gain_mix: float32 [256], replicated, may hold values from 0.1 to 1.9
- gain_ffn: float32 [256], replicated, may hold values from 0.1 to 1.9
Outputs:
- result: bfloat16 [32, 2048, 256], P('tm', 'firm')
The draws below stay inside these ranges and needn't reach their ends.
All inputs are finite; a program needn't handle non-finite values.
Results may differ from the reference program's by a relative error of at most 0.0059.
Values may be sent and summed in bfloat16 or wider, within the bound.
A program may use at most 64 MiB of HBM per device.

```python
import jax
import jax.numpy as jnp
from jax import lax

D = 256
HEADS = 4
HEAD_DIM = 64
FFN = 1024
FIRM_DEV = 256
MONTHS = 32
FIRMS = 2048
BANKS = 64
SECTORS = 32
N_FIRM = 8


def place_ends(entries, own_key, least, top_value):
    extent = entries.shape
    index_at = [jax.random.randint(jax.random.fold_in(own_key, axis), (), 0, extent[axis]) for axis in range(len(extent))]
    entries = entries.at[tuple(index_at)].set(least)
    longest = extent.index(max(extent))
    index_at[longest] = (index_at[longest] + 1) % extent[longest]
    return entries.at[tuple(index_at)].set(top_value)


def block_scale(rng, dims, split, least, largest):
    def one(dim, blocks):
        steps = jax.random.uniform(jax.random.fold_in(jax.random.fold_in(rng, 6), dim), (blocks,), jnp.float32, least / len(split), largest / len(split))
        return jnp.repeat(jnp.exp(steps), dims[dim] // blocks).reshape((-1,) + (1,) * (len(dims) - dim - 1))

    level = one(*split[0])
    for cut in split[1:]:
        level = level * one(*cut)
    return level


def gaussian(key, dims, spread, reach, cuts=(), held_as=jnp.bfloat16):
    factor_of = block_scale(key, dims, cuts, -0.22, 0.18) if cuts else 1.0
    entries = jax.random.normal(key, dims, jnp.float32) * spread * factor_of
    return jnp.minimum(jnp.maximum(entries, -reach), reach).astype(held_as)


def setup_inputs(seed: int = 0) -> dict:
    key_list = jax.random.split(jax.random.key(seed), 16)
    return {
        "features": gaussian(key_list[0], (MONTHS, FIRMS, D), 1.0, 6.0, ((0, 4), (1, 8))),
        "supply_counts": place_ends(jax.random.randint(key_list[1], (MONTHS, FIRMS, 3, FIRM_DEV), 0, 4), jax.random.fold_in(key_list[1], 1), 0, 3).astype(jnp.int32),
        "bank_ids": place_ends(jax.random.randint(key_list[2], (MONTHS, FIRMS), 0, BANKS), jax.random.fold_in(key_list[2], 1), 0, BANKS - 1).astype(jnp.int32),
        "sector_ids": place_ends(jax.random.randint(key_list[3], (MONTHS, FIRMS), 0, SECTORS), jax.random.fold_in(key_list[3], 1), 0, SECTORS - 1).astype(jnp.int32),
        "bank_table": gaussian(key_list[4], (BANKS, D), 1.0, 6.0, ((0, 8),)),
        "sector_table": gaussian(key_list[5], (SECTORS, D), 1.0, 6.0, ((0, 8),)),
        "w_supply": gaussian(key_list[6], (D, D), D ** -0.5, 0.375),
        "w_query": gaussian(key_list[7], (D, D), D ** -0.5, 0.375),
        "w_key": gaussian(key_list[8], (D, D), D ** -0.5, 0.375),
        "w_value": gaussian(key_list[9], (D, D), D ** -0.5, 0.375),
        "w_out": gaussian(key_list[10], (D, D), D ** -0.5, 0.375),
        "w_in": gaussian(key_list[11], (D, FFN), D ** -0.5, 0.375),
        "w_down": gaussian(key_list[12], (FFN, D), FFN ** -0.5, 0.1875),
        "gain_mix": jnp.clip(1.0 + 0.18 * jax.random.normal(key_list[13], (D,), jnp.float32), 0.1, 1.9),
        "gain_ffn": jnp.clip(1.0 + 0.18 * jax.random.normal(key_list[14], (D,), jnp.float32), 0.1, 1.9),
    }


def rms_norm(values, gain):
    scale = lax.rsqrt(lax.optimization_barrier(jnp.mean(values * values, axis=-1, keepdims=True)) + 1e-06)
    return values * scale * gain.astype(jnp.float32)

def reference(features, supply_counts, bank_ids, sector_ids, bank_table, sector_table, w_supply, w_query, w_key, w_value, w_out, w_in, w_down, gain_mix, gain_ffn):

    def month_step(item):
        feats, counts, banks, sectors = item
        supplied = jnp.dot(feats, w_supply, preferred_element_type=jnp.float32).astype(jnp.bfloat16)
        blocks = supplied.reshape(N_FIRM, FIRM_DEV, D)
        padded = jnp.pad(blocks, ((1, 1), (0, 0), (0, 0)))
        window = jnp.concatenate([padded[0:N_FIRM], padded[1:N_FIRM + 1], padded[2:N_FIRM + 2]], axis=1)
        tiles = counts.reshape(N_FIRM, FIRM_DEV, 3 * FIRM_DEV).astype(jnp.float32)
        message = jnp.einsum('pfs,psd->pfd', tiles, window.astype(jnp.float32)).reshape(FIRMS, D)
        degree = 1.0 + lax.optimization_barrier(jnp.sum(counts, axis=(1, 2))).astype(jnp.float32)
        message = message / jnp.sqrt(degree)[:, None]
        hub = bank_table[banks].astype(jnp.float32) + sector_table[sectors].astype(jnp.float32)
        mixed = feats.astype(jnp.float32) + message + hub
        normed = rms_norm(mixed, gain_mix).astype(jnp.bfloat16)
        query = jnp.dot(normed, w_query, preferred_element_type=jnp.float32).astype(jnp.bfloat16)
        key = jnp.dot(normed, w_key, preferred_element_type=jnp.float32).astype(jnp.bfloat16)
        value = jnp.dot(normed, w_value, preferred_element_type=jnp.float32).astype(jnp.bfloat16)
        return (mixed, query, key, value)
    mixed, query, key, value = lax.map(month_step, (features, supply_counts, bank_ids, sector_ids))

    def by_block(array):
        return jnp.swapaxes(array.reshape(MONTHS, N_FIRM, FIRM_DEV, D), 0, 1)

    def block_step(item):
        mixed_b, query_b, key_b, value_b = item
        query4 = query_b.reshape(MONTHS, FIRM_DEV, HEADS, HEAD_DIM).astype(jnp.float32)
        key_pad = jnp.pad(key_b, ((3, 0), (0, 0), (0, 0)))
        value_pad = jnp.pad(value_b, ((3, 0), (0, 0), (0, 0)))
        months_idx = jnp.arange(MONTHS, dtype=jnp.int32)
        total = jnp.zeros((MONTHS, FIRM_DEV, HEADS, HEAD_DIM), jnp.float32)
        for lag in range(4):
            key_l = key_pad[3 - lag:3 - lag + MONTHS].reshape(MONTHS, FIRM_DEV, HEADS, HEAD_DIM).astype(jnp.float32)
            value_l = value_pad[3 - lag:3 - lag + MONTHS].reshape(MONTHS, FIRM_DEV, HEADS, HEAD_DIM).astype(jnp.float32)
            score = jnp.einsum('mfhd,mfhd->mfh', query4, key_l) / jnp.sqrt(jnp.float32(HEAD_DIM)) - jnp.log(jnp.float32(4.0))
            valid = (months_idx - lag >= 0).astype(jnp.float32)[:, None, None]
            total = total + (jax.nn.sigmoid(score) * valid)[..., None] * value_l
        attended = total.astype(jnp.bfloat16).reshape(MONTHS * FIRM_DEV, D)
        second = mixed_b.reshape(MONTHS * FIRM_DEV, D) + jnp.dot(attended, w_out, preferred_element_type=jnp.float32)
        normed2 = rms_norm(second, gain_ffn).astype(jnp.bfloat16)
        inner = jax.nn.gelu(jnp.dot(normed2, w_in, preferred_element_type=jnp.float32)).astype(jnp.bfloat16)
        final = second + jnp.dot(inner, w_down, preferred_element_type=jnp.float32)
        return final.astype(jnp.bfloat16).reshape(MONTHS, FIRM_DEV, D)
    blocks_out = lax.map(block_step, (by_block(mixed), by_block(query), by_block(key), by_block(value)))
    return jnp.swapaxes(blocks_out, 0, 1).reshape(MONTHS, FIRMS, D)
```

```python
import functools
import math

import jax
import jax.numpy as jnp
from jax import lax
from jax.experimental import pallas as pl
from jax.experimental.pallas import tpu as pltpu
from jax.sharding import PartitionSpec as P

HEADS = 4
LAGS = 3
AHEAD = 3
MESH = pl.DeviceIdType.MESH
F32 = jnp.float32
BF16 = jnp.bfloat16


def dot(a, b):
    return jnp.dot(a, b, preferred_element_type=F32)


def rms_norm(values, gain):
    scale = lax.rsqrt(jnp.mean(values * values, axis=-1, keepdims=True) + 1e-06)
    return values * scale * gain


def kernel(
    groups,
    owners,
    features,
    counts_hbm,
    bank_ids,
    sector_ids,
    bank_table,
    sector_table,
    w_supply,
    w_query,
    w_key,
    w_value,
    w_out,
    w_in,
    w_down,
    gain_mix,
    gain_ffn,
    result,
    counts,
    hub_own,
    hub,
    supplied,
    direct,
    relay,
    normed_out,
    normed_in,
    query,
    key,
    value,
    mixed,
    head_sum,
    counts_sem,
    hub_send,
    hub_recv,
    direct_send,
    direct_recv,
    relay_send,
    relay_recv,
    edge_send,
    edge_recv,
):
    months, firms, width = features.shape
    banks, sectors = bank_table.shape[0], sector_table.shape[0]
    slot = hub.shape[1]
    me, group = lax.axis_index("firm"), lax.axis_index("tm")
    even = lax.rem(me, 2) == 0
    partner = jnp.where(even, me + 1, me - 1)
    target = jnp.where(even, me + 2, me - 2)
    source = jnp.where(even, me - 2, me + 2)
    sends_on = jnp.logical_and(target >= 0, target < owners)
    gets_on = jnp.logical_and(source >= 0, source < owners)
    k_direct = jnp.where(even, 2, 0)
    k_relay = 2 - k_direct
    has_before, has_after = group > 0, group < groups - 1

    def month_at(step):
        return lax.rem(step + months - LAGS, months)

    def counts_copy(m):
        return pltpu.make_async_copy(counts_hbm.at[m], counts.at[m], counts_sem.at[m])

    def direct_copy(m):
        return pltpu.make_async_remote_copy(
            src_ref=supplied.at[m],
            dst_ref=direct.at[m],
            send_sem=direct_send.at[m],
            recv_sem=direct_recv.at[m],
            device_id={"firm": partner},
            device_id_type=MESH,
        )

    def relay_copy(m):
        return pltpu.make_async_remote_copy(
            src_ref=direct.at[m],
            dst_ref=relay.at[m],
            send_sem=relay_send.at[m],
            recv_sem=relay_recv.at[m],
            device_id={"firm": target},
            device_id_type=MESH,
        )

    def edge_copy(e):
        return pltpu.make_async_remote_copy(
            src_ref=normed_out.at[e],
            dst_ref=normed_in.at[e],
            send_sem=edge_send.at[e],
            recv_sem=edge_recv.at[e],
            device_id={"tm": group + 1},
            device_id_type=MESH,
        )

    def hub_copy(shift, owner):
        return pltpu.make_async_remote_copy(
            src_ref=hub.at[owner],
            dst_ref=hub.at[owner],
            send_sem=hub_send.at[shift],
            recv_sem=hub_recv.at[owner],
            device_id={"firm": lax.rem(me + shift, owners)},
            device_id_type=MESH,
        )

    barrier = pltpu.get_barrier_semaphore()

    @pl.loop(1, owners)
    def _(shift):
        pl.semaphore_signal(
            barrier, inc=1, device_id={"firm": lax.rem(me + shift, owners)}, device_id_type=MESH
        )

    @pl.when(has_before)
    def _():
        pl.semaphore_signal(barrier, inc=1, device_id={"tm": group - 1}, device_id_type=MESH)

    @pl.when(has_after)
    def _():
        pl.semaphore_signal(barrier, inc=1, device_id={"tm": group + 1}, device_id_type=MESH)

    @pl.loop(0, months)
    def _(step):
        counts_copy(month_at(step)).start()

    @pl.loop(0, months)
    def _(step):
        m = month_at(step)
        supplied[m] = dot(features[m], w_supply[...]).astype(BF16)

    hub_own[...] = jnp.zeros_like(hub_own)
    hub_own[0:banks] = bank_table[...].astype(F32)
    hub_own[banks : banks + sectors] = sector_table[...].astype(F32)
    hub[me] = hub_own[...].astype(BF16)

    row = lax.broadcasted_iota(jnp.int32, (width, width), 0)
    column = lax.broadcasted_iota(jnp.int32, (width, width), 1)
    size = width // HEADS
    same = row // size == column // size
    head_sum[...] = jnp.where(same, 0.5 / math.sqrt(size), 0.0).astype(BF16)

    @pl.when(jnp.logical_not(gets_on))
    def _():
        relay[...] = jnp.zeros_like(relay)

    @pl.when(jnp.logical_not(has_before))
    def _():
        normed_in[...] = jnp.zeros_like(normed_in)

    pl.semaphore_wait(
        barrier, owners - 1 + has_before.astype(jnp.int32) + has_after.astype(jnp.int32)
    )

    @pl.loop(1, owners)
    def _(shift):
        hub_copy(shift, me).start()

    @pl.loop(0, AHEAD)
    def _(step):
        direct_copy(month_at(step)).start()

    def pass_on(step):
        m = month_at(step)
        direct_copy(m).wait_recv()

        @pl.when(sends_on)
        def _():
            relay_copy(m).start()

        @pl.when(step + AHEAD < months)
        def _():
            direct_copy(month_at(step + AHEAD)).start()

    hub_rows = owners * slot
    hub_row = lax.broadcasted_iota(jnp.int32, (hub_rows, firms), 0)
    place = hub_row % slot
    bank_code = jnp.where(place < banks, hub_row // slot * banks + place, -1)
    sector_code = jnp.where(
        jnp.logical_and(place >= banks, place < banks + sectors),
        hub_row // slot * sectors + place - banks,
        -1,
    )

    def mix(step):
        m = month_at(step)
        counts_copy(m).wait()

        @pl.when(gets_on)
        def _():
            relay_copy(m).wait_recv()

        own = counts[m, 1].astype(F32)
        near = counts[m, k_direct].astype(F32)
        far = counts[m, k_relay].astype(F32)
        degree = 1.0 + jnp.sum(own + near + far, axis=-1, keepdims=True)
        message = dot(own.astype(BF16), supplied[m])
        message += dot(near.astype(BF16), direct[m])
        message += dot(far.astype(BF16), relay[m])
        chosen = jnp.logical_or(
            bank_code == bank_ids[pl.ds(m, 1), :], sector_code == sector_ids[pl.ds(m, 1), :]
        )
        hubs = lax.dot_general(
            jnp.where(chosen, 1.0, 0.0).astype(BF16),
            hub[...].reshape(hub_rows, width),
            (((0,), (0,)), ((), ())),
            preferred_element_type=F32,
        )
        total = features[m].astype(F32) + message * lax.rsqrt(degree) + hubs
        mixed[m] = total
        normed = rms_norm(total, gain_mix[...]).astype(BF16)
        query[m] = dot(normed, w_query[...]).astype(BF16)
        key[m + LAGS] = dot(normed, w_key[...]).astype(BF16)
        value[m + LAGS] = dot(normed, w_value[...]).astype(BF16)
        return normed

    def finish(m):
        q = query[m]
        total = jnp.zeros((firms, width), F32)
        for lag in range(LAGS + 1):
            score = dot(q * key[m + LAGS - lag], head_sum[...]) - 0.5 * math.log(4.0)
            total += (jnp.tanh(score) + 1.0) * value[m + LAGS - lag].astype(F32)
        second = mixed[m] + dot((0.5 * total).astype(BF16), w_out[...])
        normed = rms_norm(second, gain_ffn[...]).astype(BF16)
        hidden = w_in.shape[1]
        for part in range(0, hidden, width):
            x = dot(normed, w_in[:, part : part + width])
            inner = 0.5 * x * (1.0 + jnp.tanh(math.sqrt(2.0 / math.pi) * (x + 0.044715 * x * x * x)))
            second += dot(inner.astype(BF16), w_down[part : part + width, :])
        result[m] = second.astype(BF16)

    pass_on(0)

    @pl.loop(1, owners)
    def _(shift):
        hub_copy(shift, lax.rem(me + shift, owners)).wait_recv()

    @pl.loop(0, LAGS)
    def _(step):
        pass_on(step + 1)
        normed_out[step] = mix(step)

        @pl.when(has_after)
        def _():
            edge_copy(step).start()

    @pl.loop(0, LAGS)
    def _(e):
        @pl.when(has_before)
        def _():
            edge_copy(e).wait_recv()

        key[e] = dot(normed_in[e], w_key[...]).astype(BF16)
        value[e] = dot(normed_in[e], w_value[...]).astype(BF16)

    @pl.loop(LAGS, months - 1)
    def _(step):
        pass_on(step + 1)
        mix(step)
        finish(step - LAGS)

    mix(months - 1)

    @pl.loop(months - 1 - LAGS, months)
    def _(m):
        finish(m)

    @pl.loop(1, owners)
    def _(shift):
        hub_copy(shift, me).wait_send()

    @pl.loop(0, months)
    def _(m):
        direct_copy(m).wait_send()

        @pl.when(sends_on)
        def _():
            relay_copy(m).wait_send()

    @pl.when(has_after)
    def _():
        @pl.loop(0, LAGS)
        def _(e):
            edge_copy(e).wait_send()


def body(groups, owners, features, supply_counts, bank_ids, sector_ids, bank_table, sector_table, *rest):
    *weights, gain_mix, gain_ffn = rest
    months, firms, width = features.shape
    slot = -(-(bank_table.shape[0] + sector_table.shape[0]) // 16) * 16
    block = (months, firms, width)
    halo = (LAGS, firms, width)
    vmem = pl.BlockSpec(memory_space=pltpu.VMEM)
    dma = pltpu.SemaphoreType.DMA
    rows = months * firms
    return pl.pallas_call(
        functools.partial(kernel, groups, owners),
        out_shape=jax.ShapeDtypeStruct(block, BF16),
        in_specs=[vmem, pl.BlockSpec(memory_space=pl.ANY)] + [vmem] * 13,
        out_specs=vmem,
        scratch_shapes=[
            pltpu.VMEM((months, 3, firms, firms), jnp.int32),
            pltpu.VMEM((slot, width), F32),
            pltpu.VMEM((owners, slot, width), BF16),
            pltpu.VMEM(block, BF16),
            pltpu.VMEM(block, BF16),
            pltpu.VMEM(block, BF16),
            pltpu.VMEM(halo, BF16),
            pltpu.VMEM(halo, BF16),
            pltpu.VMEM(block, BF16),
            pltpu.VMEM((months + LAGS, firms, width), BF16),
            pltpu.VMEM((months + LAGS, firms, width), BF16),
            pltpu.VMEM(block, F32),
            pltpu.VMEM((width, width), BF16),
            dma((months,)),
            dma((owners,)),
            dma((owners,)),
            dma((months,)),
            dma((months,)),
            dma((months,)),
            dma((months,)),
            dma((LAGS,)),
            dma((LAGS,)),
        ],
        compiler_params=pltpu.CompilerParams(
            collective_id=0, has_side_effects=True, vmem_limit_bytes=56 * 1024 * 1024
        ),
        cost_estimate=pl.CostEstimate(
            flops=2 * rows * width * (width * 5 + 3 * firms + 8 * width),
            bytes_accessed=rows * (3 * firms * 4 + 4 * width),
            transcendentals=rows * width * 8,
        ),
    )(
        features,
        jnp.transpose(supply_counts, (0, 2, 1, 3)),
        bank_ids,
        sector_ids,
        bank_table,
        sector_table,
        *weights,
        gain_mix.reshape(1, width),
        gain_ffn.reshape(1, width),
    )


def solution(mesh):
    in_specs = (
        P("tm", "firm", None),
        P("tm", "firm", None, None),
        P("tm", "firm"),
        P("tm", "firm"),
        P("firm", None),
        P("firm", None),
    ) + (P(),) * 9
    return jax.shard_map(
        functools.partial(body, mesh.shape["tm"], mesh.shape["firm"]),
        mesh=mesh,
        in_specs=in_specs,
        out_specs=P("tm", "firm", None),
        check_vma=False,
    )
```

```python
import functools
import math

import jax
import jax.numpy as jnp
from jax import lax
from jax.experimental import pallas as pl
from jax.experimental.pallas import tpu as pltpu
from jax.sharding import PartitionSpec as P

HEADS = 4
LAGS = 3
AHEAD = 3
HALVES = 2
MESH = pl.DeviceIdType.MESH
F32 = jnp.float32
BF16 = jnp.bfloat16


def dot(a, b):
    return jnp.dot(a, b, preferred_element_type=F32)


def rms_norm(values, gain):
    scale = lax.rsqrt(jnp.mean(values * values, axis=-1, keepdims=True) + 1e-06)
    return values * scale * gain


def kernel(
    groups,
    owners,
    features_hbm,
    counts_hbm,
    bank_ids,
    sector_ids,
    bank_table,
    sector_table,
    w_supply_hbm,
    w_query_hbm,
    w_key_hbm,
    w_value_hbm,
    w_out_hbm,
    w_in_hbm,
    w_down_hbm,
    gain_mix,
    gain_ffn,
    result_hbm,
    features,
    w_supply,
    w_query,
    w_key,
    w_value,
    w_out,
    w_in,
    w_down,
    result,
    counts,
    hub_own,
    hub,
    supplied,
    direct,
    relay,
    normed_out,
    normed_in,
    query,
    key,
    value,
    mixed,
    head_sum,
    load_sem,
    result_sem,
    counts_sem,
    hub_send,
    hub_recv,
    direct_send,
    direct_recv,
    relay_send,
    relay_recv,
    edge_send,
    edge_recv,
):
    months, firms, width = features.shape
    banks, sectors = bank_table.shape[0], sector_table.shape[0]
    slot = hub.shape[1]
    me, group = lax.axis_index("firm"), lax.axis_index("tm")
    even = lax.rem(me, 2) == 0
    partner = jnp.where(even, me + 1, me - 1)
    target = jnp.where(even, me + 2, me - 2)
    source = jnp.where(even, me - 2, me + 2)
    sends_on = jnp.logical_and(target >= 0, target < owners)
    gets_on = jnp.logical_and(source >= 0, source < owners)
    k_direct = jnp.where(even, 2, 0)
    k_relay = 2 - k_direct
    has_before, has_after = group > 0, group < groups - 1

    def month_at(step):
        return lax.rem(step + months - LAGS, months)

    def counts_copy(m):
        return pltpu.make_async_copy(counts_hbm.at[m], counts.at[m], counts_sem.at[m])

    def result_copy(m):
        return pltpu.make_async_copy(result.at[m], result_hbm.at[m], result_sem.at[m])

    loads = [
        pltpu.make_async_copy(src, dst, load_sem.at[i])
        for i, (src, dst) in enumerate(
            [
                (w_supply_hbm, w_supply),
                (features_hbm, features),
                (w_query_hbm, w_query),
                (w_key_hbm, w_key),
                (w_value_hbm, w_value),
                (w_out_hbm, w_out),
                (w_in_hbm, w_in),
                (w_down_hbm, w_down),
            ]
        )
    ]
    half = firms // HALVES

    def direct_copy(m, h):
        return pltpu.make_async_remote_copy(
            src_ref=supplied.at[m, pl.ds(h * half, half)],
            dst_ref=direct.at[m, pl.ds(h * half, half)],
            send_sem=direct_send.at[m * HALVES + h],
            recv_sem=direct_recv.at[m * HALVES + h],
            device_id={"firm": partner},
            device_id_type=MESH,
        )

    def relay_copy(m, h):
        return pltpu.make_async_remote_copy(
            src_ref=direct.at[m, pl.ds(h * half, half)],
            dst_ref=relay.at[m, pl.ds(h * half, half)],
            send_sem=relay_send.at[m * HALVES + h],
            recv_sem=relay_recv.at[m * HALVES + h],
            device_id={"firm": target},
            device_id_type=MESH,
        )

    def edge_copy(e):
        return pltpu.make_async_remote_copy(
            src_ref=normed_out.at[e],
            dst_ref=normed_in.at[e],
            send_sem=edge_send.at[e],
            recv_sem=edge_recv.at[e],
            device_id={"tm": group + 1},
            device_id_type=MESH,
        )

    def hub_copy(shift, owner):
        return pltpu.make_async_remote_copy(
            src_ref=hub.at[owner],
            dst_ref=hub.at[owner],
            send_sem=hub_send.at[shift],
            recv_sem=hub_recv.at[owner],
            device_id={"firm": lax.rem(me + shift, owners)},
            device_id_type=MESH,
        )

    barrier = pltpu.get_barrier_semaphore()

    @pl.loop(1, owners)
    def _(shift):
        pl.semaphore_signal(
            barrier, inc=1, device_id={"firm": lax.rem(me + shift, owners)}, device_id_type=MESH
        )

    @pl.when(has_before)
    def _():
        pl.semaphore_signal(barrier, inc=1, device_id={"tm": group - 1}, device_id_type=MESH)

    @pl.when(has_after)
    def _():
        pl.semaphore_signal(barrier, inc=1, device_id={"tm": group + 1}, device_id_type=MESH)

    for load in loads[:2]:
        load.start()

    @pl.loop(0, months)
    def _(step):
        counts_copy(month_at(step)).start()

    for load in loads[2:]:
        load.start()

    hub_own[...] = jnp.zeros_like(hub_own)
    hub_own[0:banks] = bank_table[...].astype(F32)
    hub_own[banks : banks + sectors] = sector_table[...].astype(F32)
    hub[me] = hub_own[...].astype(BF16)

    row = lax.broadcasted_iota(jnp.int32, (width, width), 0)
    column = lax.broadcasted_iota(jnp.int32, (width, width), 1)
    size = width // HEADS
    same = row // size == column // size
    head_sum[...] = jnp.where(same, 0.5 / math.sqrt(size), 0.0).astype(BF16)

    for load in loads[:2]:
        load.wait()
    for low, high in ((months - LAGS, months), (0, months - LAGS)):
        rows = features[low:high].reshape((high - low) * firms, width)
        supplied[low:high] = (
            dot(rows, w_supply[...]).astype(BF16).reshape(high - low, firms, width)
        )

    @pl.when(jnp.logical_not(gets_on))
    def _():
        relay[...] = jnp.zeros_like(relay)

    @pl.when(jnp.logical_not(has_before))
    def _():
        normed_in[...] = jnp.zeros_like(normed_in)

    pl.semaphore_wait(
        barrier, owners - 1 + has_before.astype(jnp.int32) + has_after.astype(jnp.int32)
    )

    @pl.loop(1, owners)
    def _(shift):
        hub_copy(shift, me).start()

    @pl.loop(0, AHEAD)
    def _(step):
        for h in range(HALVES):
            direct_copy(month_at(step), h).start()

    for load in loads[2:]:
        load.wait()

    def pass_on(step):
        m = month_at(step)

        @pl.when(step + AHEAD < months)
        def _():
            for h in range(HALVES):
                direct_copy(month_at(step + AHEAD), h).start()

        for h in range(HALVES):
            direct_copy(m, h).wait_recv()

            @pl.when(sends_on)
            def _():
                relay_copy(m, h).start()

    hub_rows = owners * slot
    hub_row = lax.broadcasted_iota(jnp.int32, (hub_rows, firms), 0)
    place = hub_row % slot
    bank_code = jnp.where(place < banks, hub_row // slot * banks + place, -1)
    sector_code = jnp.where(
        jnp.logical_and(place >= banks, place < banks + sectors),
        hub_row // slot * sectors + place - banks,
        -1,
    )

    def mix(step):
        m = month_at(step)
        counts_copy(m).wait()
        own = counts[m, 1].astype(F32)
        near = counts[m, k_direct].astype(F32)
        far = counts[m, k_relay].astype(F32)
        scale = lax.rsqrt(1.0 + jnp.sum(own + near + far, axis=-1, keepdims=True))
        message = dot(own.astype(BF16), supplied[m])
        message += dot(near.astype(BF16), direct[m])
        chosen = jnp.logical_or(
            bank_code == bank_ids[pl.ds(m, 1), :], sector_code == sector_ids[pl.ds(m, 1), :]
        )
        hubs = lax.dot_general(
            jnp.where(chosen, 1.0, 0.0).astype(BF16),
            hub[...].reshape(hub_rows, width),
            (((0,), (0,)), ((), ())),
            preferred_element_type=F32,
        )
        mixed[m] = features[m].astype(F32) + message * scale + hubs

        @pl.when(gets_on)
        def _():
            for h in range(HALVES):
                relay_copy(m, h).wait_recv()

        total = mixed[m] + dot(counts[m, k_relay].astype(F32).astype(BF16), relay[m]) * scale
        mixed[m] = total
        normed = rms_norm(total, gain_mix[...]).astype(BF16)
        query[m] = dot(normed, w_query[...]).astype(BF16)
        key[m + LAGS] = dot(normed, w_key[...]).astype(BF16)
        value[m + LAGS] = dot(normed, w_value[...]).astype(BF16)
        return normed

    def finish(first, span):
        rows = span * firms

        def block(ref, start):
            return ref[pl.ds(start, span)].reshape(rows, width)

        q = block(query, first)
        pairs = [q * block(key, first + LAGS - lag) for lag in range(LAGS + 1)]
        scores = dot(jnp.concatenate(pairs, axis=0), head_sum[...]) - 0.5 * math.log(4.0)
        total = jnp.zeros((rows, width), F32)
        for lag in range(LAGS + 1):
            weight = jnp.tanh(scores[lag * rows : (lag + 1) * rows]) + 1.0
            total += weight * block(value, first + LAGS - lag).astype(F32)
        second = block(mixed, first) + dot((0.5 * total).astype(BF16), w_out[...])
        normed = rms_norm(second, gain_ffn[...]).astype(BF16)
        hidden = w_in.shape[1]
        for part in range(0, hidden, width):
            x = dot(normed, w_in[:, part : part + width])
            inner = 0.5 * x * (1.0 + jnp.tanh(math.sqrt(2.0 / math.pi) * (x + 0.044715 * x * x * x)))
            second += dot(inner.astype(BF16), w_down[part : part + width, :])
        result[pl.ds(first, span)] = second.astype(BF16).reshape(span, firms, width)
        for i in range(span):
            result_copy(first + i).start()

    pass_on(0)

    @pl.loop(1, owners)
    def _(shift):
        hub_copy(shift, lax.rem(me + shift, owners)).wait_recv()

    @pl.loop(0, LAGS)
    def _(step):
        pass_on(step + 1)
        normed_out[step] = mix(step)

        @pl.when(has_after)
        def _():
            edge_copy(step).start()

    @pl.loop(0, LAGS)
    def _(e):
        @pl.when(has_before)
        def _():
            edge_copy(e).wait_recv()

        key[e] = dot(normed_in[e], w_key[...]).astype(BF16)
        value[e] = dot(normed_in[e], w_value[...]).astype(BF16)

    @pl.loop(LAGS, months - 1)
    def _(step):
        pass_on(step + 1)
        mix(step)
        finish(step - LAGS, 1)

    mix(months - 1)

    finish(months - 1 - LAGS, LAGS + 1)

    @pl.loop(1, owners)
    def _(shift):
        hub_copy(shift, me).wait_send()

    @pl.loop(0, months)
    def _(m):
        for h in range(HALVES):
            direct_copy(m, h).wait_send()

        @pl.when(sends_on)
        def _():
            for h in range(HALVES):
                relay_copy(m, h).wait_send()

        result_copy(m).wait()

    @pl.when(has_after)
    def _():
        @pl.loop(0, LAGS)
        def _(e):
            edge_copy(e).wait_send()


def copy_kernel(source, result, sem):
    copies = [
        pltpu.make_async_copy(source.at[m], result.at[m], sem.at[m])
        for m in range(source.shape[0])
    ]
    for copy in copies:
        copy.start()
    for copy in copies:
        copy.wait()


def body(groups, owners, features, supply_counts, bank_ids, sector_ids, bank_table, sector_table, *rest):
    *weights, gain_mix, gain_ffn = rest
    months, firms, width = features.shape
    slot = -(-(bank_table.shape[0] + sector_table.shape[0]) // 16) * 16
    block = (months, firms, width)
    halo = (LAGS, firms, width)
    vmem = pl.BlockSpec(memory_space=pltpu.VMEM)
    dma = pltpu.SemaphoreType.DMA
    rows = months * firms
    hbm = pl.BlockSpec(memory_space=pl.ANY)
    hidden = weights[-1].shape[0]
    square = pltpu.VMEM((width, width), BF16)
    out = pl.pallas_call(
        functools.partial(kernel, groups, owners),
        out_shape=jax.ShapeDtypeStruct(block, BF16),
        in_specs=[hbm] * 2 + [vmem] * 4 + [hbm] * 7 + [vmem] * 2,
        out_specs=hbm,
        scratch_shapes=[
            pltpu.VMEM(block, BF16),
            square,
            square,
            square,
            square,
            square,
            pltpu.VMEM((width, hidden), BF16),
            pltpu.VMEM((hidden, width), BF16),
            pltpu.VMEM(block, BF16),
            pltpu.VMEM((months, 3, firms, firms), jnp.int32),
            pltpu.VMEM((slot, width), F32),
            pltpu.VMEM((owners, slot, width), BF16),
            pltpu.VMEM(block, BF16),
            pltpu.VMEM(block, BF16),
            pltpu.VMEM(block, BF16),
            pltpu.VMEM(halo, BF16),
            pltpu.VMEM(halo, BF16),
            pltpu.VMEM(block, BF16),
            pltpu.VMEM((months + LAGS, firms, width), BF16),
            pltpu.VMEM((months + LAGS, firms, width), BF16),
            pltpu.VMEM(block, F32),
            pltpu.VMEM((width, width), BF16),
            dma((8,)),
            dma((months,)),
            dma((months,)),
            dma((owners,)),
            dma((owners,)),
            dma((HALVES * months,)),
            dma((HALVES * months,)),
            dma((HALVES * months,)),
            dma((HALVES * months,)),
            dma((LAGS,)),
            dma((LAGS,)),
        ],
        compiler_params=pltpu.CompilerParams(
            collective_id=0, has_side_effects=True, vmem_limit_bytes=56 * 1024 * 1024
        ),
        cost_estimate=pl.CostEstimate(
            flops=2 * rows * width * (width * 5 + 3 * firms + 8 * width),
            bytes_accessed=rows * (3 * firms * 4 + 4 * width),
            transcendentals=rows * width * 8,
        ),
    )(
        features,
        jnp.transpose(supply_counts, (0, 2, 1, 3)),
        bank_ids,
        sector_ids,
        bank_table,
        sector_table,
        *weights,
        gain_mix.reshape(1, width),
        gain_ffn.reshape(1, width),
    )
    return pl.pallas_call(
        copy_kernel,
        out_shape=jax.ShapeDtypeStruct(block, BF16),
        in_specs=[pl.BlockSpec(memory_space=pltpu.HBM)],
        out_specs=pl.BlockSpec(memory_space=pltpu.HBM),
        scratch_shapes=[dma((months,))],
        compiler_params=pltpu.CompilerParams(vmem_limit_bytes=56 * 1024 * 1024),
    )(out)


def solution(mesh):
    in_specs = (
        P("tm", "firm", None),
        P("tm", "firm", None, None),
        P("tm", "firm"),
        P("tm", "firm"),
        P("firm", None),
        P("firm", None),
    ) + (P(),) * 9
    return jax.shard_map(
        functools.partial(body, mesh.shape["tm"], mesh.shape["firm"]),
        mesh=mesh,
        in_specs=in_specs,
        out_specs=P("tm", "firm", None),
        check_vma=False,
    )
```

```python
import functools
import math

import jax
import jax.numpy as jnp
from jax import lax
from jax.experimental import pallas as pl
from jax.experimental.pallas import tpu as pltpu
from jax.sharding import PartitionSpec as P

HEADS = 4
LAGS = 3
AHEAD = 3
HALVES = 2
CURVE = math.sqrt(2.0 / math.pi)
MESH = pl.DeviceIdType.MESH
F32 = jnp.float32
BF16 = jnp.bfloat16


def dot(a, b):
    return jnp.dot(a, b, preferred_element_type=F32)


def rms_norm(values, gain):
    scale = lax.rsqrt(jnp.mean(values * values, axis=-1, keepdims=True) + 1e-06)
    return values * scale * gain


def kernel(
    groups,
    owners,
    features_hbm,
    counts_hbm,
    bank_ids,
    sector_ids,
    bank_table,
    sector_table,
    w_supply_hbm,
    w_query_hbm,
    w_key_hbm,
    w_value_hbm,
    w_out_hbm,
    w_in_hbm,
    w_down_hbm,
    gain_mix,
    gain_ffn,
    result,
    features,
    w_supply,
    w_query,
    w_key,
    w_value,
    w_out,
    w_in,
    w_down,
    counts,
    hub_own,
    hub,
    supplied,
    direct,
    relay,
    normed_out,
    normed_in,
    query,
    key,
    value,
    mixed,
    head_sum,
    load_sem,
    counts_sem,
    hub_send,
    hub_recv,
    direct_send,
    direct_recv,
    relay_send,
    relay_recv,
    edge_send,
    edge_recv,
):
    months, firms, width = features.shape
    banks, sectors = bank_table.shape[0], sector_table.shape[0]
    slot = hub.shape[1]
    me, group = lax.axis_index("firm"), lax.axis_index("tm")
    even = lax.rem(me, 2) == 0
    partner = jnp.where(even, me + 1, me - 1)
    target = jnp.where(even, me + 2, me - 2)
    source = jnp.where(even, me - 2, me + 2)
    sends_on = jnp.logical_and(target >= 0, target < owners)
    gets_on = jnp.logical_and(source >= 0, source < owners)
    k_direct = jnp.where(even, 2, 0)
    k_relay = 2 - k_direct
    has_before, has_after = group > 0, group < groups - 1

    def month_at(step):
        return lax.rem(step + months - LAGS, months)

    def counts_copy(m):
        return pltpu.make_async_copy(counts_hbm.at[m], counts.at[m], counts_sem.at[m])

    loads = [
        pltpu.make_async_copy(src, dst, load_sem.at[i])
        for i, (src, dst) in enumerate(
            [
                (w_supply_hbm, w_supply),
                (features_hbm.at[months - LAGS : months], features.at[months - LAGS : months]),
                (features_hbm.at[0 : months - LAGS], features.at[0 : months - LAGS]),
                (w_query_hbm, w_query),
                (w_key_hbm, w_key),
                (w_value_hbm, w_value),
                (w_out_hbm, w_out),
                (w_in_hbm, w_in),
                (w_down_hbm, w_down),
            ]
        )
    ]
    half = firms // HALVES

    def direct_copy(m, h):
        return pltpu.make_async_remote_copy(
            src_ref=supplied.at[m, pl.ds(h * half, half)],
            dst_ref=direct.at[m, pl.ds(h * half, half)],
            send_sem=direct_send.at[m * HALVES + h],
            recv_sem=direct_recv.at[m * HALVES + h],
            device_id={"firm": partner},
            device_id_type=MESH,
        )

    def relay_copy(m, h):
        return pltpu.make_async_remote_copy(
            src_ref=direct.at[m, pl.ds(h * half, half)],
            dst_ref=relay.at[m, pl.ds(h * half, half)],
            send_sem=relay_send.at[m * HALVES + h],
            recv_sem=relay_recv.at[m * HALVES + h],
            device_id={"firm": target},
            device_id_type=MESH,
        )

    def edge_copy(e):
        return pltpu.make_async_remote_copy(
            src_ref=normed_out.at[e],
            dst_ref=normed_in.at[e],
            send_sem=edge_send.at[e],
            recv_sem=edge_recv.at[e],
            device_id={"tm": group + 1},
            device_id_type=MESH,
        )

    def hub_copy(shift, owner):
        return pltpu.make_async_remote_copy(
            src_ref=hub.at[owner],
            dst_ref=hub.at[owner],
            send_sem=hub_send.at[shift],
            recv_sem=hub_recv.at[owner],
            device_id={"firm": lax.rem(me + shift, owners)},
            device_id_type=MESH,
        )

    barrier = pltpu.get_barrier_semaphore()

    @pl.loop(1, owners)
    def _(shift):
        pl.semaphore_signal(
            barrier, inc=1, device_id={"firm": lax.rem(me + shift, owners)}, device_id_type=MESH
        )

    @pl.when(has_before)
    def _():
        pl.semaphore_signal(barrier, inc=1, device_id={"tm": group - 1}, device_id_type=MESH)

    @pl.when(has_after)
    def _():
        pl.semaphore_signal(barrier, inc=1, device_id={"tm": group + 1}, device_id_type=MESH)

    for load in loads[:3]:
        load.start()

    @pl.loop(0, months)
    def _(step):
        counts_copy(month_at(step)).start()

    for load in loads[3:]:
        load.start()

    def supply(low, high):
        rows = features[low:high].reshape((high - low) * firms, width)
        supplied[low:high] = (
            dot(rows, w_supply[...]).astype(BF16).reshape(high - low, firms, width)
        )

    for load in loads[:2]:
        load.wait()
    supply(months - LAGS, months)
    pl.semaphore_wait(
        barrier, owners - 1 + has_before.astype(jnp.int32) + has_after.astype(jnp.int32)
    )

    @pl.loop(0, AHEAD)
    def _(step):
        for h in range(HALVES):
            direct_copy(month_at(step), h).start()

    hub_own[...] = jnp.zeros_like(hub_own)
    hub_own[0:banks] = bank_table[...].astype(F32)
    hub_own[banks : banks + sectors] = sector_table[...].astype(F32)
    hub[me] = hub_own[...].astype(BF16)

    @pl.loop(1, owners)
    def _(shift):
        hub_copy(shift, me).start()

    loads[2].wait()
    supply(0, months - LAGS)

    row = lax.broadcasted_iota(jnp.int32, (width, width), 0)
    column = lax.broadcasted_iota(jnp.int32, (width, width), 1)
    size = width // HEADS
    same = row // size == column // size
    head_sum[...] = jnp.where(same, 0.5 / math.sqrt(size), 0.0).astype(BF16)

    @pl.when(jnp.logical_not(gets_on))
    def _():
        relay[...] = jnp.zeros_like(relay)

    @pl.when(jnp.logical_not(has_before))
    def _():
        normed_in[...] = jnp.zeros_like(normed_in)

    for load in loads[3:]:
        load.wait()
    w_down[...] = w_down[...] * 0.5

    def pass_on(step):
        m = month_at(step)

        @pl.when(step + AHEAD < months)
        def _():
            for h in range(HALVES):
                direct_copy(month_at(step + AHEAD), h).start()

        for h in range(HALVES):
            direct_copy(m, h).wait_recv()

            @pl.when(sends_on)
            def _():
                relay_copy(m, h).start()

    hub_rows = owners * slot
    hub_row = lax.broadcasted_iota(jnp.int32, (hub_rows, firms), 0)
    place = hub_row % slot
    bank_code = jnp.where(place < banks, hub_row // slot * banks + place, -1)
    sector_code = jnp.where(
        jnp.logical_and(place >= banks, place < banks + sectors),
        hub_row // slot * sectors + place - banks,
        -1,
    )

    def mix(step):
        m = month_at(step)
        counts_copy(m).wait()
        own = counts[m, 1].astype(F32)
        near = counts[m, k_direct].astype(F32)
        far = counts[m, k_relay].astype(F32)
        scale = lax.rsqrt(1.0 + jnp.sum(own + near + far, axis=-1, keepdims=True))
        message = dot(own.astype(BF16), supplied[m])
        message += dot(near.astype(BF16), direct[m])
        chosen = jnp.logical_or(
            bank_code == bank_ids[pl.ds(m, 1), :], sector_code == sector_ids[pl.ds(m, 1), :]
        )
        hubs = lax.dot_general(
            jnp.where(chosen, 1.0, 0.0).astype(BF16),
            hub[...].reshape(hub_rows, width),
            (((0,), (0,)), ((), ())),
            preferred_element_type=F32,
        )
        mixed[m] = features[m].astype(F32) + message * scale + hubs

        @pl.when(gets_on)
        def _():
            for h in range(HALVES):
                relay_copy(m, h).wait_recv()

        total = mixed[m] + dot(counts[m, k_relay].astype(F32).astype(BF16), relay[m]) * scale
        mixed[m] = total
        normed = rms_norm(total, gain_mix[...]).astype(BF16)
        query[m] = dot(normed, w_query[...]).astype(BF16)
        key[m + LAGS] = dot(normed, w_key[...]).astype(BF16)
        value[m + LAGS] = dot(normed, w_value[...]).astype(BF16)
        return normed

    def finish(first, span):
        rows = span * firms

        def block(ref, start):
            return ref[pl.ds(start, span)].reshape(rows, width)

        q = block(query, first)
        pairs = [q * block(key, first + LAGS - lag) for lag in range(LAGS + 1)]
        scores = dot(jnp.concatenate(pairs, axis=0), head_sum[...]) - 0.5 * math.log(4.0)
        total = jnp.zeros((rows, width), F32)
        for lag in range(LAGS + 1):
            weight = jnp.tanh(scores[lag * rows : (lag + 1) * rows]) + 1.0
            total += weight * block(value, first + LAGS - lag).astype(F32)
        second = block(mixed, first) + dot((0.5 * total).astype(BF16), w_out[...])
        normed = rms_norm(second, gain_ffn[...]).astype(BF16)
        hidden = w_in.shape[1]
        for part in range(0, hidden, width):
            x = dot(normed, w_in[:, part : part + width])
            inner = x + x * jnp.tanh(x * (CURVE + 0.044715 * CURVE * (x * x)))
            second += dot(inner.astype(BF16), w_down[part : part + width, :])
        result[pl.ds(first, span)] = second.astype(BF16).reshape(span, firms, width)

    pass_on(0)

    @pl.loop(1, owners)
    def _(shift):
        hub_copy(shift, lax.rem(me + shift, owners)).wait_recv()

    @pl.loop(0, LAGS)
    def _(step):
        pass_on(step + 1)
        normed_out[step] = mix(step)

        @pl.when(has_after)
        def _():
            edge_copy(step).start()

    @pl.loop(0, LAGS)
    def _(e):
        @pl.when(has_before)
        def _():
            edge_copy(e).wait_recv()

        key[e] = dot(normed_in[e], w_key[...]).astype(BF16)
        value[e] = dot(normed_in[e], w_value[...]).astype(BF16)

    @pl.loop(LAGS, months - 1)
    def _(step):
        pass_on(step + 1)
        mix(step)
        finish(step - LAGS, 1)

    mix(months - 1)

    finish(months - 1 - LAGS, LAGS + 1)

    @pl.loop(1, owners)
    def _(shift):
        hub_copy(shift, me).wait_send()

    @pl.loop(0, months)
    def _(m):
        for h in range(HALVES):
            direct_copy(m, h).wait_send()

        @pl.when(sends_on)
        def _():
            for h in range(HALVES):
                relay_copy(m, h).wait_send()

    @pl.when(has_after)
    def _():
        @pl.loop(0, LAGS)
        def _(e):
            edge_copy(e).wait_send()


def copy_kernel(source, result, sem):
    copies = [
        pltpu.make_async_copy(source.at[m], result.at[m], sem.at[m])
        for m in range(source.shape[0])
    ]
    for copy in copies:
        copy.start()
    for copy in copies:
        copy.wait()


def body(groups, owners, features, supply_counts, bank_ids, sector_ids, bank_table, sector_table, *rest):
    *weights, gain_mix, gain_ffn = rest
    months, firms, width = features.shape
    slot = -(-(bank_table.shape[0] + sector_table.shape[0]) // 16) * 16
    block = (months, firms, width)
    halo = (LAGS, firms, width)
    vmem = pl.BlockSpec(memory_space=pltpu.VMEM)
    dma = pltpu.SemaphoreType.DMA
    rows = months * firms
    hbm = pl.BlockSpec(memory_space=pltpu.HBM)
    hidden = weights[-1].shape[0]
    square = pltpu.VMEM((width, width), BF16)
    out = pl.pallas_call(
        functools.partial(kernel, groups, owners),
        out_shape=jax.ShapeDtypeStruct(block, BF16),
        in_specs=[hbm] * 2 + [vmem] * 4 + [hbm] * 7 + [vmem] * 2,
        out_specs=vmem,
        scratch_shapes=[
            pltpu.VMEM(block, BF16),
            square,
            square,
            square,
            square,
            square,
            pltpu.VMEM((width, hidden), BF16),
            pltpu.VMEM((hidden, width), BF16),
            pltpu.VMEM((months, 3, firms, firms), jnp.int32),
            pltpu.VMEM((slot, width), F32),
            pltpu.VMEM((owners, slot, width), BF16),
            pltpu.VMEM(block, BF16),
            pltpu.VMEM(block, BF16),
            pltpu.VMEM(block, BF16),
            pltpu.VMEM(halo, BF16),
            pltpu.VMEM(halo, BF16),
            pltpu.VMEM(block, BF16),
            pltpu.VMEM((months + LAGS, firms, width), BF16),
            pltpu.VMEM((months + LAGS, firms, width), BF16),
            pltpu.VMEM(block, F32),
            pltpu.VMEM((width, width), BF16),
            dma((9,)),
            dma((months,)),
            dma((owners,)),
            dma((owners,)),
            dma((HALVES * months,)),
            dma((HALVES * months,)),
            dma((HALVES * months,)),
            dma((HALVES * months,)),
            dma((LAGS,)),
            dma((LAGS,)),
        ],
        compiler_params=pltpu.CompilerParams(
            collective_id=0, has_side_effects=True, vmem_limit_bytes=50 * 1024 * 1024
        ),
        cost_estimate=pl.CostEstimate(
            flops=2 * rows * width * (width * 5 + 3 * firms + 8 * width),
            bytes_accessed=rows * (3 * firms * 4 + 4 * width),
            transcendentals=rows * width * 8,
        ),
    )(
        features,
        jnp.transpose(supply_counts, (0, 2, 1, 3)),
        bank_ids,
        sector_ids,
        bank_table,
        sector_table,
        *weights,
        gain_mix.reshape(1, width),
        gain_ffn.reshape(1, width),
    )
    return pl.pallas_call(
        copy_kernel,
        out_shape=jax.ShapeDtypeStruct(block, BF16),
        in_specs=[vmem],
        out_specs=hbm,
        scratch_shapes=[dma((months,))],
    )(out)


def solution(mesh):
    in_specs = (
        P("tm", "firm", None),
        P("tm", "firm", None, None),
        P("tm", "firm"),
        P("tm", "firm"),
        P("firm", None),
        P("firm", None),
    ) + (P(),) * 9
    return jax.shard_map(
        functools.partial(body, mesh.shape["tm"], mesh.shape["firm"]),
        mesh=mesh,
        in_specs=in_specs,
        out_specs=P("tm", "firm", None),
        check_vma=False,
    )
```

```python
import functools
import math

import jax
import jax.numpy as jnp
from jax import lax
from jax.experimental import pallas as pl
from jax.experimental.pallas import tpu as pltpu
from jax.sharding import PartitionSpec as P

HEADS = 4
LAGS = 3
AHEAD = 3
HALVES = 2
CURVE = math.sqrt(2.0 / math.pi)
MESH = pl.DeviceIdType.MESH
F32 = jnp.float32
BF16 = jnp.bfloat16


def dot(a, b):
    return jnp.dot(a, b, preferred_element_type=F32)


def rms_norm(values, gain):
    scale = lax.rsqrt(jnp.mean(values * values, axis=-1, keepdims=True) + 1e-06)
    return values * scale * gain


def kernel(
    groups,
    owners,
    features_hbm,
    counts_hbm,
    bank_ids,
    sector_ids,
    bank_table,
    sector_table,
    w_supply_hbm,
    w_query_hbm,
    w_key_hbm,
    w_value_hbm,
    w_out_hbm,
    w_in_hbm,
    w_down_hbm,
    gain_mix,
    gain_ffn,
    result,
    features,
    w_supply,
    w_query,
    w_key,
    w_value,
    w_out,
    w_in,
    w_down,
    counts,
    hub_own,
    hub,
    supplied,
    direct,
    relay,
    normed_out,
    normed_in,
    query,
    key,
    value,
    mixed,
    head_sum,
    load_sem,
    counts_sem,
    hub_send,
    hub_recv,
    direct_send,
    direct_recv,
    relay_send,
    relay_recv,
    edge_send,
    edge_recv,
):
    months, firms, width = features.shape
    banks, sectors = bank_table.shape[0], sector_table.shape[0]
    slot = hub.shape[1]
    me, group = lax.axis_index("firm"), lax.axis_index("tm")
    even = lax.rem(me, 2) == 0
    partner = jnp.where(even, me + 1, me - 1)
    target = jnp.where(even, me + 2, me - 2)
    source = jnp.where(even, me - 2, me + 2)
    sends_on = jnp.logical_and(target >= 0, target < owners)
    gets_on = jnp.logical_and(source >= 0, source < owners)
    k_direct = jnp.where(even, 2, 0)
    k_relay = 2 - k_direct
    has_before, has_after = group > 0, group < groups - 1

    def month_at(step):
        return lax.rem(step + months - LAGS, months)

    def counts_copy(m):
        return pltpu.make_async_copy(counts_hbm.at[m], counts.at[m], counts_sem.at[m])

    loads = [
        pltpu.make_async_copy(src, dst, load_sem.at[i])
        for i, (src, dst) in enumerate(
            [
                (w_supply_hbm, w_supply),
                (features_hbm.at[months - LAGS : months], features.at[months - LAGS : months]),
                (features_hbm.at[0 : months - LAGS], features.at[0 : months - LAGS]),
                (w_query_hbm, w_query),
                (w_key_hbm, w_key),
                (w_value_hbm, w_value),
                (w_out_hbm, w_out),
                (w_in_hbm, w_in),
                (w_down_hbm, w_down),
            ]
        )
    ]
    half = firms // HALVES

    def direct_copy(m, h):
        return pltpu.make_async_remote_copy(
            src_ref=supplied.at[m, pl.ds(h * half, half)],
            dst_ref=direct.at[m, pl.ds(h * half, half)],
            send_sem=direct_send.at[m * HALVES + h],
            recv_sem=direct_recv.at[m * HALVES + h],
            device_id={"firm": partner},
            device_id_type=MESH,
        )

    def relay_copy(m, h):
        return pltpu.make_async_remote_copy(
            src_ref=direct.at[m, pl.ds(h * half, half)],
            dst_ref=relay.at[m, pl.ds(h * half, half)],
            send_sem=relay_send.at[m * HALVES + h],
            recv_sem=relay_recv.at[m * HALVES + h],
            device_id={"firm": target},
            device_id_type=MESH,
        )

    def edge_copy(e):
        return pltpu.make_async_remote_copy(
            src_ref=normed_out.at[e],
            dst_ref=normed_in.at[e],
            send_sem=edge_send.at[e],
            recv_sem=edge_recv.at[e],
            device_id={"tm": group + 1},
            device_id_type=MESH,
        )

    def hub_copy(shift, owner):
        return pltpu.make_async_remote_copy(
            src_ref=hub.at[owner],
            dst_ref=hub.at[owner],
            send_sem=hub_send.at[shift],
            recv_sem=hub_recv.at[owner],
            device_id={"firm": lax.rem(me + shift, owners)},
            device_id_type=MESH,
        )

    barrier = pltpu.get_barrier_semaphore()

    @pl.loop(1, owners)
    def _(shift):
        pl.semaphore_signal(
            barrier, inc=1, device_id={"firm": lax.rem(me + shift, owners)}, device_id_type=MESH
        )

    @pl.when(has_before)
    def _():
        pl.semaphore_signal(barrier, inc=1, device_id={"tm": group - 1}, device_id_type=MESH)

    @pl.when(has_after)
    def _():
        pl.semaphore_signal(barrier, inc=1, device_id={"tm": group + 1}, device_id_type=MESH)

    for load in loads[:3]:
        load.start()

    @pl.loop(0, months)
    def _(step):
        counts_copy(month_at(step)).start()

    for load in loads[3:]:
        load.start()

    def supply(low, high):
        rows = features[low:high].reshape((high - low) * firms, width)
        supplied[low:high] = (
            dot(rows, w_supply[...]).astype(BF16).reshape(high - low, firms, width)
        )

    for load in loads[:2]:
        load.wait()
    supply(months - LAGS, months)
    pl.semaphore_wait(
        barrier, owners - 1 + has_before.astype(jnp.int32) + has_after.astype(jnp.int32)
    )

    @pl.loop(0, AHEAD)
    def _(step):
        for h in range(HALVES):
            direct_copy(month_at(step), h).start()

    hub_own[...] = jnp.zeros_like(hub_own)
    hub_own[0:banks] = bank_table[...].astype(F32)
    hub_own[banks : banks + sectors] = sector_table[...].astype(F32)
    hub[me] = hub_own[...].astype(BF16)

    @pl.loop(1, owners)
    def _(shift):
        hub_copy(shift, me).start()

    loads[2].wait()
    supply(0, months - LAGS)

    row = lax.broadcasted_iota(jnp.int32, (width, width), 0)
    column = lax.broadcasted_iota(jnp.int32, (width, width), 1)
    size = width // HEADS
    same = row // size == column // size
    head_sum[...] = jnp.where(same, 0.5 / math.sqrt(size), 0.0).astype(BF16)

    @pl.when(jnp.logical_not(gets_on))
    def _():
        relay[...] = jnp.zeros_like(relay)

    @pl.when(jnp.logical_not(has_before))
    def _():
        normed_in[...] = jnp.zeros_like(normed_in)

    for load in loads[3:]:
        load.wait()
    w_down[...] = w_down[...] * 0.5

    def pass_on(step):
        m = month_at(step)

        @pl.when(step + AHEAD < months)
        def _():
            for h in range(HALVES):
                direct_copy(month_at(step + AHEAD), h).start()

        for h in range(HALVES):
            direct_copy(m, h).wait_recv()

            @pl.when(sends_on)
            def _():
                relay_copy(m, h).start()

    hub_rows = owners * slot
    hub_row = lax.broadcasted_iota(jnp.int32, (hub_rows, firms), 0)
    place = hub_row % slot
    bank_code = jnp.where(place < banks, hub_row // slot * banks + place, -1)
    sector_code = jnp.where(
        jnp.logical_and(place >= banks, place < banks + sectors),
        hub_row // slot * sectors + place - banks,
        -1,
    )

    def mix(step):
        m = month_at(step)
        counts_copy(m).wait()
        own = counts[m, 1].astype(F32)
        near = counts[m, k_direct].astype(F32)
        far = counts[m, k_relay].astype(F32)
        scale = lax.rsqrt(1.0 + jnp.sum(own + near + far, axis=-1, keepdims=True))
        message = dot(own.astype(BF16), supplied[m])
        message += dot(near.astype(BF16), direct[m])
        chosen = jnp.logical_or(
            bank_code == bank_ids[pl.ds(m, 1), :], sector_code == sector_ids[pl.ds(m, 1), :]
        )
        hubs = lax.dot_general(
            jnp.where(chosen, 1.0, 0.0).astype(BF16),
            hub[...].reshape(hub_rows, width),
            (((0,), (0,)), ((), ())),
            preferred_element_type=F32,
        )
        mixed[m] = features[m].astype(F32) + message * scale + hubs

        @pl.when(gets_on)
        def _():
            for h in range(HALVES):
                relay_copy(m, h).wait_recv()

        total = mixed[m] + dot(counts[m, k_relay].astype(F32).astype(BF16), relay[m]) * scale
        mixed[m] = total
        normed = rms_norm(total, gain_mix[...]).astype(BF16)
        query[m] = dot(normed, w_query[...]).astype(BF16)
        key[m + LAGS] = dot(normed, w_key[...]).astype(BF16)
        value[m + LAGS] = dot(normed, w_value[...]).astype(BF16)
        return normed

    def finish(first, span):
        rows = span * firms

        def block(ref, start):
            return ref[pl.ds(start, span)].reshape(rows, width)

        q = block(query, first)
        pairs = [q * block(key, first + LAGS - lag) for lag in range(LAGS + 1)]
        scores = dot(jnp.concatenate(pairs, axis=0), head_sum[...]) - 0.5 * math.log(4.0)
        total = jnp.zeros((rows, width), F32)
        for lag in range(LAGS + 1):
            weight = jnp.tanh(scores[lag * rows : (lag + 1) * rows]) + 1.0
            total += weight * block(value, first + LAGS - lag).astype(F32)
        second = block(mixed, first) + dot((0.5 * total).astype(BF16), w_out[...])
        normed = rms_norm(second, gain_ffn[...]).astype(BF16)
        inner = []
        for part in range(0, w_in.shape[1], width):
            x = dot(normed, w_in[:, part : part + width]).astype(BF16)
            curve = x * (BF16(CURVE) + BF16(0.044715 * CURVE) * (x * x))
            inner.append(x + x * jnp.tanh(curve))
        second += dot(jnp.concatenate(inner, axis=1), w_down[...])
        result[pl.ds(first, span)] = second.astype(BF16).reshape(span, firms, width)

    pass_on(0)

    @pl.loop(1, owners)
    def _(shift):
        hub_copy(shift, lax.rem(me + shift, owners)).wait_recv()

    @pl.loop(0, LAGS)
    def _(step):
        pass_on(step + 1)
        normed_out[step] = mix(step)

        @pl.when(has_after)
        def _():
            edge_copy(step).start()

    @pl.loop(0, LAGS)
    def _(e):
        @pl.when(has_before)
        def _():
            edge_copy(e).wait_recv()

        key[e] = dot(normed_in[e], w_key[...]).astype(BF16)
        value[e] = dot(normed_in[e], w_value[...]).astype(BF16)

    @pl.loop(LAGS, months - 1)
    def _(step):
        pass_on(step + 1)
        mix(step)
        finish(step - LAGS, 1)

    mix(months - 1)

    finish(months - 1 - LAGS, LAGS + 1)

    @pl.loop(1, owners)
    def _(shift):
        hub_copy(shift, me).wait_send()

    @pl.loop(0, months)
    def _(m):
        for h in range(HALVES):
            direct_copy(m, h).wait_send()

        @pl.when(sends_on)
        def _():
            for h in range(HALVES):
                relay_copy(m, h).wait_send()

    @pl.when(has_after)
    def _():
        @pl.loop(0, LAGS)
        def _(e):
            edge_copy(e).wait_send()


def body(groups, owners, features, supply_counts, bank_ids, sector_ids, bank_table, sector_table, *rest):
    *weights, gain_mix, gain_ffn = rest
    months, firms, width = features.shape
    slot = -(-(bank_table.shape[0] + sector_table.shape[0]) // 16) * 16
    block = (months, firms, width)
    halo = (LAGS, firms, width)
    vmem = pl.BlockSpec(memory_space=pltpu.VMEM)
    dma = pltpu.SemaphoreType.DMA
    rows = months * firms
    hbm = pl.BlockSpec(memory_space=pltpu.HBM)
    hidden = weights[-1].shape[0]
    square = pltpu.VMEM((width, width), BF16)
    return pl.pallas_call(
        functools.partial(kernel, groups, owners),
        out_shape=jax.ShapeDtypeStruct(block, BF16),
        in_specs=[hbm] * 2 + [vmem] * 4 + [hbm] * 7 + [vmem] * 2,
        out_specs=vmem,
        scratch_shapes=[
            pltpu.VMEM(block, BF16),
            square,
            square,
            square,
            square,
            square,
            pltpu.VMEM((width, hidden), BF16),
            pltpu.VMEM((hidden, width), BF16),
            pltpu.VMEM((months, 3, firms, firms), jnp.int32),
            pltpu.VMEM((slot, width), F32),
            pltpu.VMEM((owners, slot, width), BF16),
            pltpu.VMEM(block, BF16),
            pltpu.VMEM(block, BF16),
            pltpu.VMEM(block, BF16),
            pltpu.VMEM(halo, BF16),
            pltpu.VMEM(halo, BF16),
            pltpu.VMEM(block, BF16),
            pltpu.VMEM((months + LAGS, firms, width), BF16),
            pltpu.VMEM((months + LAGS, firms, width), BF16),
            pltpu.VMEM(block, F32),
            pltpu.VMEM((width, width), BF16),
            dma((9,)),
            dma((months,)),
            dma((owners,)),
            dma((owners,)),
            dma((HALVES * months,)),
            dma((HALVES * months,)),
            dma((HALVES * months,)),
            dma((HALVES * months,)),
            dma((LAGS,)),
            dma((LAGS,)),
        ],
        compiler_params=pltpu.CompilerParams(
            collective_id=0, has_side_effects=True, vmem_limit_bytes=56 * 1024 * 1024
        ),
        cost_estimate=pl.CostEstimate(
            flops=2 * rows * width * (width * 5 + 3 * firms + 8 * width),
            bytes_accessed=rows * (3 * firms * 4 + 4 * width),
            transcendentals=rows * width * 8,
        ),
    )(
        features,
        jnp.transpose(supply_counts, (0, 2, 1, 3)),
        bank_ids,
        sector_ids,
        bank_table,
        sector_table,
        *weights,
        gain_mix.reshape(1, width),
        gain_ffn.reshape(1, width),
    )


def solution(mesh):
    in_specs = (
        P("tm", "firm", None),
        P("tm", "firm", None, None),
        P("tm", "firm"),
        P("tm", "firm"),
        P("firm", None),
        P("firm", None),
    ) + (P(),) * 9
    return jax.shard_map(
        functools.partial(body, mesh.shape["tm"], mesh.shape["firm"]),
        mesh=mesh,
        in_specs=in_specs,
        out_specs=P("tm", "firm", None),
        check_vma=False,
    )
```

```python
import functools
import math

import jax
import jax.numpy as jnp
from jax import lax
from jax.experimental import pallas as pl
from jax.experimental.pallas import tpu as pltpu
from jax.sharding import PartitionSpec as P

HEADS = 4
LAGS = 3
AHEAD = 3
HALVES = 2
CURVE = math.sqrt(2.0 / math.pi)
MESH = pl.DeviceIdType.MESH
F32 = jnp.float32
BF16 = jnp.bfloat16


def dot(a, b):
    return jnp.dot(a, b, preferred_element_type=F32)


def rms_norm(values, gain):
    scale = lax.rsqrt(jnp.mean(values * values, axis=-1, keepdims=True) + 1e-06)
    return values * scale * gain


def kernel(
    groups,
    owners,
    features_hbm,
    counts_hbm,
    bank_ids,
    sector_ids,
    bank_table,
    sector_table,
    w_supply_hbm,
    w_query_hbm,
    w_key_hbm,
    w_value_hbm,
    w_out_hbm,
    w_in_hbm,
    w_down_hbm,
    gain_mix,
    gain_ffn,
    result_hbm,
    features,
    w_supply,
    w_query,
    w_key,
    w_value,
    w_out,
    w_in,
    w_down,
    result,
    counts,
    hub_own,
    hub,
    supplied,
    direct,
    relay,
    normed_out,
    normed_in,
    query,
    key,
    value,
    mixed,
    head_sum,
    load_sem,
    result_sem,
    counts_sem,
    hub_send,
    hub_recv,
    direct_send,
    direct_recv,
    relay_send,
    relay_recv,
    edge_send,
    edge_recv,
):
    months, firms, width = features.shape
    banks, sectors = bank_table.shape[0], sector_table.shape[0]
    slot = hub.shape[1]
    me, group = lax.axis_index("firm"), lax.axis_index("tm")
    even = lax.rem(me, 2) == 0
    partner = jnp.where(even, me + 1, me - 1)
    target = jnp.where(even, me + 2, me - 2)
    source = jnp.where(even, me - 2, me + 2)
    sends_on = jnp.logical_and(target >= 0, target < owners)
    gets_on = jnp.logical_and(source >= 0, source < owners)
    k_direct = jnp.where(even, 2, 0)
    k_relay = 2 - k_direct
    has_before, has_after = group > 0, group < groups - 1

    def month_at(step):
        return lax.rem(step + months - LAGS, months)

    def counts_copy(m):
        return pltpu.make_async_copy(counts_hbm.at[m], counts.at[m], counts_sem.at[m])

    def result_copy(m):
        return pltpu.make_async_copy(result.at[m], result_hbm.at[m], result_sem.at[m])

    loads = [
        pltpu.make_async_copy(src, dst, load_sem.at[i])
        for i, (src, dst) in enumerate(
            [
                (w_supply_hbm, w_supply),
                (features_hbm.at[months - LAGS : months], features.at[months - LAGS : months]),
                (features_hbm.at[0 : months - LAGS], features.at[0 : months - LAGS]),
                (w_query_hbm, w_query),
                (w_key_hbm, w_key),
                (w_value_hbm, w_value),
                (w_out_hbm, w_out),
                (w_in_hbm, w_in),
                (w_down_hbm, w_down),
            ]
        )
    ]
    half = firms // HALVES

    def direct_copy(m, h):
        return pltpu.make_async_remote_copy(
            src_ref=supplied.at[m, pl.ds(h * half, half)],
            dst_ref=direct.at[m, pl.ds(h * half, half)],
            send_sem=direct_send.at[m * HALVES + h],
            recv_sem=direct_recv.at[m * HALVES + h],
            device_id={"firm": partner},
            device_id_type=MESH,
        )

    def relay_copy(m, h):
        return pltpu.make_async_remote_copy(
            src_ref=direct.at[m, pl.ds(h * half, half)],
            dst_ref=relay.at[m, pl.ds(h * half, half)],
            send_sem=relay_send.at[m * HALVES + h],
            recv_sem=relay_recv.at[m * HALVES + h],
            device_id={"firm": target},
            device_id_type=MESH,
        )

    def edge_copy(e):
        return pltpu.make_async_remote_copy(
            src_ref=normed_out.at[e],
            dst_ref=normed_in.at[e],
            send_sem=edge_send.at[e],
            recv_sem=edge_recv.at[e],
            device_id={"tm": group + 1},
            device_id_type=MESH,
        )

    def hub_copy(shift, owner):
        return pltpu.make_async_remote_copy(
            src_ref=hub.at[owner],
            dst_ref=hub.at[owner],
            send_sem=hub_send.at[shift],
            recv_sem=hub_recv.at[owner],
            device_id={"firm": lax.rem(me + shift, owners)},
            device_id_type=MESH,
        )

    barrier = pltpu.get_barrier_semaphore()

    @pl.loop(1, owners)
    def _(shift):
        pl.semaphore_signal(
            barrier, inc=1, device_id={"firm": lax.rem(me + shift, owners)}, device_id_type=MESH
        )

    @pl.when(has_before)
    def _():
        pl.semaphore_signal(barrier, inc=1, device_id={"tm": group - 1}, device_id_type=MESH)

    @pl.when(has_after)
    def _():
        pl.semaphore_signal(barrier, inc=1, device_id={"tm": group + 1}, device_id_type=MESH)

    for load in loads[:3]:
        load.start()

    @pl.loop(0, months)
    def _(step):
        counts_copy(month_at(step)).start()

    for load in loads[3:]:
        load.start()

    def supply(low, high):
        rows = features[low:high].reshape((high - low) * firms, width)
        supplied[low:high] = (
            dot(rows, w_supply[...]).astype(BF16).reshape(high - low, firms, width)
        )

    for load in loads[:2]:
        load.wait()
    supply(months - LAGS, months)
    pl.semaphore_wait(
        barrier, owners - 1 + has_before.astype(jnp.int32) + has_after.astype(jnp.int32)
    )

    @pl.loop(0, AHEAD)
    def _(step):
        for h in range(HALVES):
            direct_copy(month_at(step), h).start()

    hub_own[...] = jnp.zeros_like(hub_own)
    hub_own[0:banks] = bank_table[...].astype(F32)
    hub_own[banks : banks + sectors] = sector_table[...].astype(F32)
    hub[me] = hub_own[...].astype(BF16)

    @pl.loop(1, owners)
    def _(shift):
        hub_copy(shift, me).start()

    loads[2].wait()
    supply(0, months - LAGS)

    row = lax.broadcasted_iota(jnp.int32, (width, width), 0)
    column = lax.broadcasted_iota(jnp.int32, (width, width), 1)
    size = width // HEADS
    same = row // size == column // size
    head_sum[...] = jnp.where(same, 0.5 / math.sqrt(size), 0.0).astype(BF16)

    @pl.when(jnp.logical_not(gets_on))
    def _():
        relay[...] = jnp.zeros_like(relay)

    @pl.when(jnp.logical_not(has_before))
    def _():
        normed_in[...] = jnp.zeros_like(normed_in)

    for load in loads[3:]:
        load.wait()
    w_down[...] = w_down[...] * 0.5

    def pass_on(step):
        m = month_at(step)

        @pl.when(step + AHEAD < months)
        def _():
            for h in range(HALVES):
                direct_copy(month_at(step + AHEAD), h).start()

        for h in range(HALVES):
            direct_copy(m, h).wait_recv()

            @pl.when(sends_on)
            def _():
                relay_copy(m, h).start()

    hub_rows = owners * slot
    hub_row = lax.broadcasted_iota(jnp.int32, (hub_rows, firms), 0)
    place = hub_row % slot
    bank_code = jnp.where(place < banks, hub_row // slot * banks + place, -1)
    sector_code = jnp.where(
        jnp.logical_and(place >= banks, place < banks + sectors),
        hub_row // slot * sectors + place - banks,
        -1,
    )

    def mix(step):
        m = month_at(step)
        counts_copy(m).wait()
        own = counts[m, 1].astype(F32)
        near = counts[m, k_direct].astype(F32)
        far = counts[m, k_relay].astype(F32)
        scale = lax.rsqrt(1.0 + jnp.sum(own + near + far, axis=-1, keepdims=True))
        message = dot(own.astype(BF16), supplied[m])
        message += dot(near.astype(BF16), direct[m])
        chosen = jnp.logical_or(
            bank_code == bank_ids[pl.ds(m, 1), :], sector_code == sector_ids[pl.ds(m, 1), :]
        )
        hubs = lax.dot_general(
            jnp.where(chosen, 1.0, 0.0).astype(BF16),
            hub[...].reshape(hub_rows, width),
            (((0,), (0,)), ((), ())),
            preferred_element_type=F32,
        )
        mixed[m] = features[m].astype(F32) + message * scale + hubs

        @pl.when(gets_on)
        def _():
            for h in range(HALVES):
                relay_copy(m, h).wait_recv()

        total = mixed[m] + dot(counts[m, k_relay].astype(F32).astype(BF16), relay[m]) * scale
        mixed[m] = total
        normed = rms_norm(total, gain_mix[...]).astype(BF16)
        query[m] = dot(normed, w_query[...]).astype(BF16)
        key[m + LAGS] = dot(normed, w_key[...]).astype(BF16)
        value[m + LAGS] = dot(normed, w_value[...]).astype(BF16)
        return normed

    def finish(first, span):
        rows = span * firms

        def block(ref, start):
            return ref[pl.ds(start, span)].reshape(rows, width)

        q = block(query, first)
        pairs = [q * block(key, first + LAGS - lag) for lag in range(LAGS + 1)]
        scores = dot(jnp.concatenate(pairs, axis=0), head_sum[...]) - 0.5 * math.log(4.0)
        total = jnp.zeros((rows, width), F32)
        for lag in range(LAGS + 1):
            weight = jnp.tanh(scores[lag * rows : (lag + 1) * rows]) + 1.0
            total += weight * block(value, first + LAGS - lag).astype(F32)
        second = block(mixed, first) + dot((0.5 * total).astype(BF16), w_out[...])
        normed = rms_norm(second, gain_ffn[...]).astype(BF16)
        inner = []
        for part in range(0, w_in.shape[1], width):
            x = dot(normed, w_in[:, part : part + width]).astype(BF16)
            curve = x * (BF16(CURVE) + BF16(0.044715 * CURVE) * (x * x))
            inner.append(x + x * jnp.tanh(curve))
        second += dot(jnp.concatenate(inner, axis=1), w_down[...])
        result[pl.ds(first, span)] = second.astype(BF16).reshape(span, firms, width)
        for i in range(span):
            result_copy(first + i).start()

    pass_on(0)

    @pl.loop(1, owners)
    def _(shift):
        hub_copy(shift, lax.rem(me + shift, owners)).wait_recv()

    @pl.loop(0, LAGS)
    def _(step):
        pass_on(step + 1)
        normed_out[step] = mix(step)

        @pl.when(has_after)
        def _():
            edge_copy(step).start()

    @pl.loop(0, LAGS)
    def _(e):
        @pl.when(has_before)
        def _():
            edge_copy(e).wait_recv()

        key[e] = dot(normed_in[e], w_key[...]).astype(BF16)
        value[e] = dot(normed_in[e], w_value[...]).astype(BF16)

    @pl.loop(LAGS, months - 1)
    def _(step):
        pass_on(step + 1)
        mix(step)
        finish(step - LAGS, 1)

    mix(months - 1)

    finish(months - 1 - LAGS, LAGS + 1)

    @pl.loop(1, owners)
    def _(shift):
        hub_copy(shift, me).wait_send()

    @pl.loop(0, months)
    def _(m):
        for h in range(HALVES):
            direct_copy(m, h).wait_send()

        @pl.when(sends_on)
        def _():
            for h in range(HALVES):
                relay_copy(m, h).wait_send()

        result_copy(m).wait()

    @pl.when(has_after)
    def _():
        @pl.loop(0, LAGS)
        def _(e):
            edge_copy(e).wait_send()


def body(groups, owners, features, supply_counts, bank_ids, sector_ids, bank_table, sector_table, *rest):
    *weights, gain_mix, gain_ffn = rest
    months, firms, width = features.shape
    slot = -(-(bank_table.shape[0] + sector_table.shape[0]) // 16) * 16
    block = (months, firms, width)
    halo = (LAGS, firms, width)
    vmem = pl.BlockSpec(memory_space=pltpu.VMEM)
    dma = pltpu.SemaphoreType.DMA
    rows = months * firms
    hbm = pl.BlockSpec(memory_space=pltpu.HBM)
    hidden = weights[-1].shape[0]
    square = pltpu.VMEM((width, width), BF16)
    return pl.pallas_call(
        functools.partial(kernel, groups, owners),
        out_shape=jax.ShapeDtypeStruct(block, BF16),
        in_specs=[hbm] * 2 + [vmem] * 4 + [hbm] * 7 + [vmem] * 2,
        out_specs=hbm,
        scratch_shapes=[
            pltpu.VMEM(block, BF16),
            square,
            square,
            square,
            square,
            square,
            pltpu.VMEM((width, hidden), BF16),
            pltpu.VMEM((hidden, width), BF16),
            pltpu.VMEM(block, BF16),
            pltpu.VMEM((months, 3, firms, firms), jnp.int32),
            pltpu.VMEM((slot, width), F32),
            pltpu.VMEM((owners, slot, width), BF16),
            pltpu.VMEM(block, BF16),
            pltpu.VMEM(block, BF16),
            pltpu.VMEM(block, BF16),
            pltpu.VMEM(halo, BF16),
            pltpu.VMEM(halo, BF16),
            pltpu.VMEM(block, BF16),
            pltpu.VMEM((months + LAGS, firms, width), BF16),
            pltpu.VMEM((months + LAGS, firms, width), BF16),
            pltpu.VMEM(block, F32),
            pltpu.VMEM((width, width), BF16),
            dma((9,)),
            dma((months,)),
            dma((months,)),
            dma((owners,)),
            dma((owners,)),
            dma((HALVES * months,)),
            dma((HALVES * months,)),
            dma((HALVES * months,)),
            dma((HALVES * months,)),
            dma((LAGS,)),
            dma((LAGS,)),
        ],
        compiler_params=pltpu.CompilerParams(
            collective_id=0, has_side_effects=True, vmem_limit_bytes=56 * 1024 * 1024
        ),
        cost_estimate=pl.CostEstimate(
            flops=2 * rows * width * (width * 5 + 3 * firms + 8 * width),
            bytes_accessed=rows * (3 * firms * 4 + 4 * width),
            transcendentals=rows * width * 8,
        ),
    )(
        features,
        jnp.transpose(supply_counts, (0, 2, 1, 3)),
        bank_ids,
        sector_ids,
        bank_table,
        sector_table,
        *weights,
        gain_mix.reshape(1, width),
        gain_ffn.reshape(1, width),
    )


def solution(mesh):
    in_specs = (
        P("tm", "firm", None),
        P("tm", "firm", None, None),
        P("tm", "firm"),
        P("tm", "firm"),
        P("firm", None),
        P("firm", None),
    ) + (P(),) * 9
    return jax.shard_map(
        functools.partial(body, mesh.shape["tm"], mesh.shape["firm"]),
        mesh=mesh,
        in_specs=in_specs,
        out_specs=P("tm", "firm", None),
        check_vma=False,
    )
```

```python
import functools
import math

import jax
import jax.numpy as jnp
from jax import lax
from jax.experimental import pallas as pl
from jax.experimental.pallas import tpu as pltpu
from jax.sharding import PartitionSpec as P

HEADS = 4
LAGS = 3
AHEAD = 3
HALVES = 4
CURVE = math.sqrt(2.0 / math.pi)
MESH = pl.DeviceIdType.MESH
F32 = jnp.float32
BF16 = jnp.bfloat16


def dot(a, b):
    return jnp.dot(a, b, preferred_element_type=F32)


def rms_norm(values, gain):
    scale = lax.rsqrt(jnp.mean(values * values, axis=-1, keepdims=True) + 1e-06)
    return values * scale * gain


def kernel(
    groups,
    owners,
    features_hbm,
    counts_hbm,
    bank_ids,
    sector_ids,
    bank_table,
    sector_table,
    w_supply_hbm,
    w_query_hbm,
    w_key_hbm,
    w_value_hbm,
    w_out_hbm,
    w_in_hbm,
    w_down_hbm,
    gain_mix,
    gain_ffn,
    result_hbm,
    features,
    w_supply,
    w_query,
    w_key,
    w_value,
    w_out,
    w_in,
    w_down,
    result,
    counts,
    hub_own,
    hub,
    supplied,
    direct,
    relay,
    normed_out,
    normed_in,
    query,
    key,
    value,
    mixed,
    head_sum,
    load_sem,
    result_sem,
    counts_sem,
    hub_send,
    hub_recv,
    direct_send,
    direct_recv,
    relay_send,
    relay_recv,
    edge_send,
    edge_recv,
):
    months, firms, width = features.shape
    banks, sectors = bank_table.shape[0], sector_table.shape[0]
    slot = hub.shape[1]
    me, group = lax.axis_index("firm"), lax.axis_index("tm")
    even = lax.rem(me, 2) == 0
    partner = jnp.where(even, me + 1, me - 1)
    target = jnp.where(even, me + 2, me - 2)
    source = jnp.where(even, me - 2, me + 2)
    sends_on = jnp.logical_and(target >= 0, target < owners)
    gets_on = jnp.logical_and(source >= 0, source < owners)
    k_direct = jnp.where(even, 2, 0)
    k_relay = 2 - k_direct
    has_before, has_after = group > 0, group < groups - 1

    def month_at(step):
        return lax.rem(step + months - LAGS, months)

    def counts_copy(m):
        return pltpu.make_async_copy(counts_hbm.at[m], counts.at[m], counts_sem.at[m])

    def result_copy(m):
        return pltpu.make_async_copy(result.at[m], result_hbm.at[m], result_sem.at[m])

    loads = [
        pltpu.make_async_copy(src, dst, load_sem.at[i])
        for i, (src, dst) in enumerate(
            [
                (w_supply_hbm, w_supply),
                (features_hbm.at[months - LAGS : months], features.at[months - LAGS : months]),
                (features_hbm.at[0 : months - LAGS], features.at[0 : months - LAGS]),
                (w_query_hbm, w_query),
                (w_key_hbm, w_key),
                (w_value_hbm, w_value),
                (w_out_hbm, w_out),
                (w_in_hbm, w_in),
                (w_down_hbm, w_down),
            ]
        )
    ]
    half = firms // HALVES

    def direct_copy(m, h):
        return pltpu.make_async_remote_copy(
            src_ref=supplied.at[m, pl.ds(h * half, half)],
            dst_ref=direct.at[m, pl.ds(h * half, half)],
            send_sem=direct_send.at[m * HALVES + h],
            recv_sem=direct_recv.at[m * HALVES + h],
            device_id={"firm": partner},
            device_id_type=MESH,
        )

    def relay_copy(m, h):
        return pltpu.make_async_remote_copy(
            src_ref=direct.at[m, pl.ds(h * half, half)],
            dst_ref=relay.at[m, pl.ds(h * half, half)],
            send_sem=relay_send.at[m * HALVES + h],
            recv_sem=relay_recv.at[m * HALVES + h],
            device_id={"firm": target},
            device_id_type=MESH,
        )

    def edge_copy(e):
        return pltpu.make_async_remote_copy(
            src_ref=normed_out.at[e],
            dst_ref=normed_in.at[e],
            send_sem=edge_send.at[e],
            recv_sem=edge_recv.at[e],
            device_id={"tm": group + 1},
            device_id_type=MESH,
        )

    def hub_copy(shift, owner):
        return pltpu.make_async_remote_copy(
            src_ref=hub.at[owner],
            dst_ref=hub.at[owner],
            send_sem=hub_send.at[shift],
            recv_sem=hub_recv.at[owner],
            device_id={"firm": lax.rem(me + shift, owners)},
            device_id_type=MESH,
        )

    barrier = pltpu.get_barrier_semaphore()

    @pl.loop(1, owners)
    def _(shift):
        pl.semaphore_signal(
            barrier, inc=1, device_id={"firm": lax.rem(me + shift, owners)}, device_id_type=MESH
        )

    @pl.when(has_before)
    def _():
        pl.semaphore_signal(barrier, inc=1, device_id={"tm": group - 1}, device_id_type=MESH)

    @pl.when(has_after)
    def _():
        pl.semaphore_signal(barrier, inc=1, device_id={"tm": group + 1}, device_id_type=MESH)

    for load in loads[:3]:
        load.start()

    @pl.loop(0, months)
    def _(step):
        counts_copy(month_at(step)).start()

    for load in loads[3:]:
        load.start()

    def supply(low, high):
        rows = features[low:high].reshape((high - low) * firms, width)
        supplied[low:high] = (
            dot(rows, w_supply[...]).astype(BF16).reshape(high - low, firms, width)
        )

    for load in loads[:2]:
        load.wait()
    supply(months - LAGS, months)
    pl.semaphore_wait(
        barrier, owners - 1 + has_before.astype(jnp.int32) + has_after.astype(jnp.int32)
    )

    @pl.loop(0, AHEAD)
    def _(step):
        for h in range(HALVES):
            direct_copy(month_at(step), h).start()

    hub_own[...] = jnp.zeros_like(hub_own)
    hub_own[0:banks] = bank_table[...].astype(F32)
    hub_own[banks : banks + sectors] = sector_table[...].astype(F32)
    hub[me] = hub_own[...].astype(BF16)

    @pl.loop(1, owners)
    def _(shift):
        hub_copy(shift, me).start()

    loads[2].wait()
    supply(0, months - LAGS)

    row = lax.broadcasted_iota(jnp.int32, (width, width), 0)
    column = lax.broadcasted_iota(jnp.int32, (width, width), 1)
    size = width // HEADS
    same = row // size == column // size
    head_sum[...] = jnp.where(same, 0.5 / math.sqrt(size), 0.0).astype(BF16)

    @pl.when(jnp.logical_not(gets_on))
    def _():
        relay[...] = jnp.zeros_like(relay)

    @pl.when(jnp.logical_not(has_before))
    def _():
        normed_in[...] = jnp.zeros_like(normed_in)

    for load in loads[3:]:
        load.wait()
    w_down[...] = w_down[...] * 0.5

    def pass_on(step):
        m = month_at(step)

        @pl.when(step + AHEAD < months)
        def _():
            for h in range(HALVES):
                direct_copy(month_at(step + AHEAD), h).start()

        for h in range(HALVES):
            direct_copy(m, h).wait_recv()

            @pl.when(sends_on)
            def _():
                relay_copy(m, h).start()

    hub_rows = owners * slot
    hub_row = lax.broadcasted_iota(jnp.int32, (hub_rows, firms), 0)
    place = hub_row % slot
    bank_code = jnp.where(place < banks, hub_row // slot * banks + place, -1)
    sector_code = jnp.where(
        jnp.logical_and(place >= banks, place < banks + sectors),
        hub_row // slot * sectors + place - banks,
        -1,
    )

    def mix(step):
        m = month_at(step)
        counts_copy(m).wait()
        own = counts[m, 1].astype(F32)
        near = counts[m, k_direct].astype(F32)
        far = counts[m, k_relay].astype(F32)
        scale = lax.rsqrt(1.0 + jnp.sum(own + near + far, axis=-1, keepdims=True))
        message = dot(own.astype(BF16), supplied[m])
        message += dot(near.astype(BF16), direct[m])
        chosen = jnp.logical_or(
            bank_code == bank_ids[pl.ds(m, 1), :], sector_code == sector_ids[pl.ds(m, 1), :]
        )
        hubs = lax.dot_general(
            jnp.where(chosen, 1.0, 0.0).astype(BF16),
            hub[...].reshape(hub_rows, width),
            (((0,), (0,)), ((), ())),
            preferred_element_type=F32,
        )
        mixed[m] = features[m].astype(F32) + message * scale + hubs

        @pl.when(gets_on)
        def _():
            for h in range(HALVES):
                relay_copy(m, h).wait_recv()

        total = mixed[m] + dot(counts[m, k_relay].astype(F32).astype(BF16), relay[m]) * scale
        mixed[m] = total
        normed = rms_norm(total, gain_mix[...]).astype(BF16)
        query[m] = dot(normed, w_query[...]).astype(BF16)
        key[m + LAGS] = dot(normed, w_key[...]).astype(BF16)
        value[m + LAGS] = dot(normed, w_value[...]).astype(BF16)
        return normed

    def finish(first, span):
        rows = span * firms

        def block(ref, start):
            return ref[pl.ds(start, span)].reshape(rows, width)

        q = block(query, first)
        pairs = [q * block(key, first + LAGS - lag) for lag in range(LAGS + 1)]
        scores = dot(jnp.concatenate(pairs, axis=0), head_sum[...]) - 0.5 * math.log(4.0)
        total = jnp.zeros((rows, width), F32)
        for lag in range(LAGS + 1):
            weight = jnp.tanh(scores[lag * rows : (lag + 1) * rows]) + 1.0
            total += weight * block(value, first + LAGS - lag).astype(F32)
        second = block(mixed, first) + dot((0.5 * total).astype(BF16), w_out[...])
        normed = rms_norm(second, gain_ffn[...]).astype(BF16)
        inner = []
        for part in range(0, w_in.shape[1], width):
            x = dot(normed, w_in[:, part : part + width]).astype(BF16)
            curve = x * (BF16(CURVE) + BF16(0.044715 * CURVE) * (x * x))
            inner.append(x + x * jnp.tanh(curve))
        second += dot(jnp.concatenate(inner, axis=1), w_down[...])
        result[pl.ds(first, span)] = second.astype(BF16).reshape(span, firms, width)
        for i in range(span):
            result_copy(first + i).start()

    pass_on(0)

    @pl.loop(1, owners)
    def _(shift):
        hub_copy(shift, lax.rem(me + shift, owners)).wait_recv()

    @pl.loop(0, LAGS)
    def _(step):
        pass_on(step + 1)
        normed_out[step] = mix(step)

        @pl.when(has_after)
        def _():
            edge_copy(step).start()

    @pl.loop(0, LAGS)
    def _(e):
        @pl.when(has_before)
        def _():
            edge_copy(e).wait_recv()

        key[e] = dot(normed_in[e], w_key[...]).astype(BF16)
        value[e] = dot(normed_in[e], w_value[...]).astype(BF16)

    @pl.loop(LAGS, months - 1)
    def _(step):
        pass_on(step + 1)
        mix(step)
        finish(step - LAGS, 1)

    mix(months - 1)

    finish(months - 1 - LAGS, LAGS + 1)

    @pl.loop(1, owners)
    def _(shift):
        hub_copy(shift, me).wait_send()

    @pl.loop(0, months)
    def _(m):
        for h in range(HALVES):
            direct_copy(m, h).wait_send()

        @pl.when(sends_on)
        def _():
            for h in range(HALVES):
                relay_copy(m, h).wait_send()

        result_copy(m).wait()

    @pl.when(has_after)
    def _():
        @pl.loop(0, LAGS)
        def _(e):
            edge_copy(e).wait_send()


def body(groups, owners, features, supply_counts, bank_ids, sector_ids, bank_table, sector_table, *rest):
    *weights, gain_mix, gain_ffn = rest
    months, firms, width = features.shape
    slot = -(-(bank_table.shape[0] + sector_table.shape[0]) // 16) * 16
    block = (months, firms, width)
    halo = (LAGS, firms, width)
    vmem = pl.BlockSpec(memory_space=pltpu.VMEM)
    dma = pltpu.SemaphoreType.DMA
    rows = months * firms
    hbm = pl.BlockSpec(memory_space=pltpu.HBM)
    hidden = weights[-1].shape[0]
    square = pltpu.VMEM((width, width), BF16)
    return pl.pallas_call(
        functools.partial(kernel, groups, owners),
        out_shape=jax.ShapeDtypeStruct(block, BF16),
        in_specs=[hbm] * 2 + [vmem] * 4 + [hbm] * 7 + [vmem] * 2,
        out_specs=hbm,
        scratch_shapes=[
            pltpu.VMEM(block, BF16),
            square,
            square,
            square,
            square,
            square,
            pltpu.VMEM((width, hidden), BF16),
            pltpu.VMEM((hidden, width), BF16),
            pltpu.VMEM(block, BF16),
            pltpu.VMEM((months, 3, firms, firms), jnp.int32),
            pltpu.VMEM((slot, width), F32),
            pltpu.VMEM((owners, slot, width), BF16),
            pltpu.VMEM(block, BF16),
            pltpu.VMEM(block, BF16),
            pltpu.VMEM(block, BF16),
            pltpu.VMEM(halo, BF16),
            pltpu.VMEM(halo, BF16),
            pltpu.VMEM(block, BF16),
            pltpu.VMEM((months + LAGS, firms, width), BF16),
            pltpu.VMEM((months + LAGS, firms, width), BF16),
            pltpu.VMEM(block, F32),
            pltpu.VMEM((width, width), BF16),
            dma((9,)),
            dma((months,)),
            dma((months,)),
            dma((owners,)),
            dma((owners,)),
            dma((HALVES * months,)),
            dma((HALVES * months,)),
            dma((HALVES * months,)),
            dma((HALVES * months,)),
            dma((LAGS,)),
            dma((LAGS,)),
        ],
        compiler_params=pltpu.CompilerParams(
            collective_id=0, has_side_effects=True, vmem_limit_bytes=56 * 1024 * 1024
        ),
        cost_estimate=pl.CostEstimate(
            flops=2 * rows * width * (width * 5 + 3 * firms + 8 * width),
            bytes_accessed=rows * (3 * firms * 4 + 4 * width),
            transcendentals=rows * width * 8,
        ),
    )(
        features,
        jnp.transpose(supply_counts, (0, 2, 1, 3)),
        bank_ids,
        sector_ids,
        bank_table,
        sector_table,
        *weights,
        gain_mix.reshape(1, width),
        gain_ffn.reshape(1, width),
    )


def solution(mesh):
    in_specs = (
        P("tm", "firm", None),
        P("tm", "firm", None, None),
        P("tm", "firm"),
        P("tm", "firm"),
        P("firm", None),
        P("firm", None),
    ) + (P(),) * 9
    return jax.shard_map(
        functools.partial(body, mesh.shape["tm"], mesh.shape["firm"]),
        mesh=mesh,
        in_specs=in_specs,
        out_specs=P("tm", "firm", None),
        check_vma=False,
    )
```
